32 devices in a mesh: run: 16 (over z, x, core), entry: 2 (over y).
Axes of the slice: x: 2, y: 2, z: 4, core: 2. Of those that a mesh axis runs over, the one named last changes fastest.
Arguments:
- gradients: bfloat16 [8192, 65536], P('run', 'entry'), may hold values from -6 to 6
- probes: bfloat16 [65536, 512], P(('entry', 'run')), may hold values from -0.0234375 to 0.0234375
Outputs:
- projected: float32 [512, 65536], P('run', 'entry')
The draws below stay inside these ranges and needn't reach their ends.
All inputs are finite; a program needn't handle non-finite values.
Results may differ from the reference program's by a relative error of at most 0.0026.
Values may be sent and summed in bfloat16 or wider, within the bound.
A program may use at most 192 MiB of HBM per device.

```python
import jax
import jax.numpy as jnp
from jax import lax

ENTRIES = 65536
PROBES = 512
RUN_DEV = 512
RUNS = 8192


def levels(own_key, shape, pieces, smallest, high):
    factor_of = 1.0
    for position, shards_of in pieces:
        heights = jax.random.uniform(jax.random.fold_in(jax.random.fold_in(own_key, 6), position), (shards_of,), jnp.float32, smallest / len(pieces), high / len(pieces))
        factor_of = factor_of * jnp.repeat(jnp.exp(heights), shape[position] // shards_of).reshape((-1,) + (1,) * (len(shape) - 1 - position))
    return factor_of


def bell_draw(rng, dims, deviation, limit, cuts=(), kind=jnp.bfloat16):
    entries = jax.random.normal(rng, dims, jnp.float32) * deviation
    if len(cuts) > 0:
        entries = levels(rng, dims, cuts, -0.22, 0.18) * entries
    return jnp.clip(entries, min=-limit, max=limit).astype(kind)


def setup_inputs(seed: int = 0) -> dict:
    arg_keys = jax.random.split(jax.random.key(seed), 3)
    return {
        "gradients": bell_draw(arg_keys[0], (RUNS, ENTRIES), 1.0, 6.0, ((0, 16), (1, 2))),
        "probes": bell_draw(arg_keys[1], (ENTRIES, PROBES), ENTRIES ** -0.5, 0.0234375, ((0, 32),)),
    }


def reference(gradients, probes):
    blocks = gradients.reshape(RUNS // RUN_DEV, RUN_DEV, ENTRIES)

    def sketch_block(block):
        return jnp.dot(block.astype(jnp.float32), probes.astype(jnp.float32), preferred_element_type=jnp.float32)
    sketch = lax.map(sketch_block, blocks).reshape(RUNS, PROBES)
    gram = jnp.dot(sketch.T.astype(jnp.float32), sketch.astype(jnp.float32), precision=lax.Precision.HIGHEST, preferred_element_type=jnp.float32)
    factor = jnp.linalg.cholesky(gram)
    basis = lax.linalg.triangular_solve(factor, sketch, left_side=False, lower=True, transpose_a=True).astype(jnp.bfloat16)
    basis_blocks = basis.reshape(RUNS // RUN_DEV, RUN_DEV, PROBES)

    def project_block(total, pair):
        left, block = pair
        term = lax.dot_general(left.astype(jnp.float32), block.astype(jnp.float32), (((0,), (0,)), ((), ())), preferred_element_type=jnp.float32)
        return (total + term, None)
    start = jnp.zeros((PROBES, ENTRIES), jnp.float32)
    projected, unused = lax.scan(project_block, start, (basis_blocks, blocks))
    return projected
```

```python
import functools

import jax
import jax.numpy as jnp
from jax import lax
from jax.experimental import pallas as pl
from jax.experimental.pallas import tpu as pltpu
from jax.sharding import PartitionSpec as P

HIGH = lax.Precision.HIGHEST
BLOCK = 128
TILE = 256
MESH = pl.DeviceIdType.MESH


def mm(a, b, dims, precision=None):
    return lax.dot_general(
        a, b, (dims, ((), ())), precision=precision, preferred_element_type=jnp.float32
    )


def factor_blocks(gram):
    count = gram.shape[0] // BLOCK
    eye = jnp.eye(BLOCK, dtype=jnp.float32)
    low, inv = {}, []
    rest = gram
    for k in range(count):
        diag = jnp.linalg.cholesky(rest[:BLOCK, :BLOCK], symmetrize_input=False)
        inverse = lax.linalg.triangular_solve(diag, eye, left_side=True, lower=True)
        inv.append(inverse)
        if k + 1 < count:
            panel = mm(rest[BLOCK:, :BLOCK], inverse, ((1,), (1,)), HIGH)
            for j in range(k + 1, count):
                low[j, k] = panel[(j - k - 1) * BLOCK : (j - k) * BLOCK]
            rest = rest[BLOCK:, BLOCK:] - mm(panel, panel, ((1,), (1,)), HIGH)
    return low, inv


def orthonormal(sketch, gram):
    low, inv = factor_blocks(gram)
    parts = []
    for k in range(len(inv)):
        right = sketch[:, k * BLOCK : (k + 1) * BLOCK]
        if k:
            row = jnp.concatenate([low[k, j] for j in range(k)], axis=1)
            right = right - mm(jnp.concatenate(parts, axis=1), row, ((1,), (1,)), HIGH)
        parts.append(mm(right, inv[k], ((1,), (1,)), HIGH))
    return jnp.concatenate(parts, axis=1).astype(jnp.bfloat16)


def project_kernel(
    depth, away_ref, home_ref, mine_ref, theirs_ref, out_ref,
    tiles, total, outgoing, incoming, relay,
    load_sem, x_send, x_recv, z_send, z_recv, keep_sem, core_send, core_recv,
):
    me = lax.axis_index("run")
    core, z = me % 2, me // 4
    flip = me + 1 - 2 * core
    across = me + 2 - 4 * ((me // 2) % 2)
    chunks, _, band, piece = total.shape
    rows = mine_ref.shape[0]
    last = depth - 1
    part = band // 2

    barrier = pltpu.get_barrier_semaphore()
    for device in (flip, across):
        pl.semaphore_signal(barrier, inc=1, device_id={"run": device}, device_id_type=MESH)

    @pl.when(z > 0)
    def _():
        pl.semaphore_signal(barrier, inc=1, device_id={"run": me - 4}, device_id_type=MESH)

    @pl.when(z < last)
    def _():
        pl.semaphore_signal(barrier, inc=1, device_id={"run": me + 4}, device_id_type=MESH)

    pl.semaphore_wait(barrier, 2 + (z + last - 1) // last + (2 * last - 1 - z) // last)

    def loads(k, slot):
        columns = pl.ds(pl.multiple_of(k * piece, piece), piece)
        return (
            pltpu.make_async_copy(
                mine_ref.at[:, columns], tiles.at[slot, pl.ds(0, rows)], load_sem.at[slot, 0]
            ),
            pltpu.make_async_copy(
                theirs_ref.at[:, columns], tiles.at[slot, pl.ds(rows, rows)], load_sem.at[slot, 1]
            ),
        )

    def x_copy(k):
        return pltpu.make_async_remote_copy(
            src_ref=outgoing.at[k], dst_ref=incoming.at[k],
            send_sem=x_send.at[k], recv_sem=x_recv.at[k],
            device_id={"run": across}, device_id_type=MESH,
        )

    def z_copy(k, slot, device):
        return pltpu.make_async_remote_copy(
            src_ref=relay.at[k, slot], dst_ref=relay.at[k, slot],
            send_sem=z_send.at[k, slot], recv_sem=z_recv.at[k, slot],
            device_id={"run": device}, device_id_type=MESH,
        )

    def result_copies(k):
        columns = pl.ds(pl.multiple_of((2 * k + core) * piece, piece), piece)
        keep = pltpu.make_async_copy(
            total.at[k, z, pl.ds(pl.multiple_of(core * part, part), part)],
            out_ref.at[:, columns], keep_sem.at[k],
        )
        give = pltpu.make_async_remote_copy(
            src_ref=total.at[k, z, pl.ds(pl.multiple_of((1 - core) * part, part), part)],
            dst_ref=out_ref.at[:, columns],
            send_sem=core_send.at[k], recv_sem=core_recv.at[k],
            device_id={"run": flip}, device_id_type=MESH,
        )
        return keep, give

    for copy in loads(0, 0):
        copy.start()

    def multiply(k, carry):
        slot = k % 2

        @pl.when(k + 1 < chunks)
        def _():
            for copy in loads(k + 1, 1 - slot):
                copy.start()

        for copy in loads(k, slot):
            copy.wait()

        def send_tile(i, carry):
            span = pl.ds(pl.multiple_of(i * TILE, TILE), TILE)
            value = jnp.dot(
                away_ref[...], tiles[slot, :, span], preferred_element_type=jnp.float32
            ).astype(jnp.bfloat16)
            for d in range(depth):
                outgoing[k, d, :, span] = value[d * band : (d + 1) * band]
            return carry

        def keep_tile(i, carry):
            span = pl.ds(pl.multiple_of(i * TILE, TILE), TILE)
            value = jnp.dot(home_ref[...], tiles[slot, :, span], preferred_element_type=jnp.float32)
            for d in range(depth):
                total[k, d, :, span] = value[d * band : (d + 1) * band]
            return carry

        lax.fori_loop(0, piece // TILE, send_tile, 0)
        x_copy(k).start()
        lax.fori_loop(0, piece // TILE, keep_tile, 0)
        return carry

    lax.fori_loop(0, chunks, multiply, 0)

    def pass_on(k, t, dest, slot, first, source, target):
        @pl.when(first)
        def _():
            relay[k, slot] = total[k, dest].astype(jnp.bfloat16)

        @pl.when(jnp.logical_not(first))
        def _():
            z_copy(k, slot, source).wait_recv()
            relay[k, slot] = (
                total[k, dest] + relay[k, slot].astype(jnp.float32)
            ).astype(jnp.bfloat16)

        z_copy(k, slot, target).start()

    def tick(now, carry):
        @pl.when(now < chunks)
        def _():
            x_copy(now).wait_recv()
            for d in range(depth):
                total[now, d] = total[now, d] + incoming[now, d].astype(jnp.float32)

        for t in range(last):
            k = now - t
            live = jnp.logical_and(k >= 0, k < chunks)

            @pl.when(jnp.logical_and(live, z <= t))
            def _():
                dest = last - t + z
                pass_on(k, t, dest, dest + 1, z == 0, me - 4, me + 4)

            @pl.when(jnp.logical_and(live, last - z <= t))
            def _():
                dest = t - last + z
                pass_on(k, t, dest, dest, z == last, me + 4, me - 4)

        @pl.when(now >= last)
        def _():
            k = now - last

            @pl.when(z > 0)
            def _():
                z_copy(k, z + 1, me - 4).wait_recv()
                total[k, z] = total[k, z] + relay[k, z + 1].astype(jnp.float32)

            @pl.when(z < last)
            def _():
                z_copy(k, z, me + 4).wait_recv()
                total[k, z] = total[k, z] + relay[k, z].astype(jnp.float32)

            for copy in result_copies(k):
                copy.start()

        return carry

    lax.fori_loop(0, chunks + last, tick, 0)

    def drain(k, carry):
        x_copy(k).wait_send()
        for t in range(last):
            @pl.when(z <= t)
            def _():
                z_copy(k, last - t + z + 1, me + 4).wait_send()

            @pl.when(last - z <= t)
            def _():
                z_copy(k, t - last + z, me - 4).wait_send()

        keep, give = result_copies(k)
        keep.wait()
        give.wait()
        return carry

    lax.fori_loop(0, chunks, drain, 0)


def project(depth, away, home, mine, theirs, piece):
    width, both = away.shape
    rows, columns = mine.shape
    chunks, band = columns // piece, width // depth
    any_space, vmem = pl.BlockSpec(memory_space=pl.ANY), pl.BlockSpec(memory_space=pltpu.VMEM)
    dma = pltpu.SemaphoreType.DMA
    return pl.pallas_call(
        functools.partial(project_kernel, depth),
        out_shape=jax.ShapeDtypeStruct((band // 2, 2 * columns), jnp.float32),
        in_specs=[vmem, vmem, any_space, any_space],
        out_specs=any_space,
        scratch_shapes=[
            pltpu.VMEM((2, both, piece), jnp.bfloat16),
            pltpu.VMEM((chunks, depth, band, piece), jnp.float32),
            pltpu.VMEM((chunks, depth, band, piece), jnp.bfloat16),
            pltpu.VMEM((chunks, depth, band, piece), jnp.bfloat16),
            pltpu.VMEM((chunks, depth + 1, band, piece), jnp.bfloat16),
            dma((2, 2)), dma((chunks,)), dma((chunks,)),
            dma((chunks, depth + 1)), dma((chunks, depth + 1)),
            dma((chunks,)), dma((chunks,)), dma((chunks,)),
        ],
        compiler_params=pltpu.CompilerParams(
            collective_id=0, has_side_effects=True, vmem_limit_bytes=60 * 2**20
        ),
        cost_estimate=pl.CostEstimate(
            flops=4 * width * both * columns, bytes_accessed=4 * rows * columns, transcendentals=0
        ),
    )(away, home, mine, theirs)


def solution(mesh):
    runs, entries = mesh.shape["run"], mesh.shape["entry"]
    depth = runs // 4

    def swap(value, bit, axis="run"):
        size = mesh.shape[axis]
        return lax.ppermute(value, axis, [(i, i ^ bit) for i in range(size)])

    def butterfly(value, axis):
        bit = 1
        while bit < mesh.shape[axis]:
            value = value + swap(value, bit, axis)
            bit *= 2
        return value

    def per_device(gradients, probes):
        me = lax.axis_index("run")
        core, x, z = me % 2, (me // 2) % 2, me // 4
        rows, columns = gradients.shape
        piece, width = probes.shape
        halves = runs // 2

        def columns_of(c):
            return jnp.concatenate(
                [
                    lax.dynamic_slice_in_dim(gradients, (2 * j + c) * piece, piece, 1)
                    for j in range(halves)
                ],
                axis=1,
            )

        theirs = swap(columns_of(1 - core), 1)
        mine = columns_of(core)
        groups = [list(range(c, runs, 2)) for c in range(2)]
        table = lax.all_gather(probes, "run", axis=0, tiled=True, axis_index_groups=groups)
        other = swap(mm(theirs, table, ((1,), (0,))), 1)
        sketch = mm(mine, table, ((1,), (0,))) + other
        sketch = butterfly(sketch, "entry")
        part = lax.axis_index("entry") % 2
        half = lax.dynamic_slice_in_dim(sketch, part * (width // 2), width // 2, 1)
        gram_half = butterfly(mm(sketch, half, ((0,), (0,)), HIGH), "run")
        far_half = swap(gram_half, 1, "entry")
        gram = jnp.concatenate(
            [
                jnp.where(part == 0, gram_half, far_half),
                jnp.where(part == 0, far_half, gram_half),
            ],
            axis=1,
        )
        basis = orthonormal(sketch, gram)
        basis_theirs = swap(basis, 1)

        band = width // depth // 2

        def bands(value, which):
            value = value.reshape(rows, depth, 2, band)
            return lax.dynamic_index_in_dim(value, which, 2, keepdims=False).reshape(
                rows, depth * band
            )

        both = jnp.concatenate
        away = both([bands(basis, 1 - x), bands(basis_theirs, 1 - x)]).T
        home = both([bands(basis, x), bands(basis_theirs, x)]).T
        return project(depth, away, home, mine, theirs, piece)

    placed = (P("run", "entry"), P(("entry", "run"), None))
    return jax.shard_map(
        per_device, mesh=mesh, in_specs=placed, out_specs=P("run", "entry"), check_vma=False
    )
```

```python
import functools

import jax
import jax.numpy as jnp
from jax import lax
from jax.experimental import pallas as pl
from jax.experimental.pallas import tpu as pltpu
from jax.sharding import PartitionSpec as P

HIGH = lax.Precision.HIGHEST
BLOCK = 128
TILE = 256
MESH = pl.DeviceIdType.MESH


def mm(a, b, dims, precision=None):
    return lax.dot_general(
        a, b, (dims, ((), ())), precision=precision, preferred_element_type=jnp.float32
    )


def factor_blocks(gram):
    count = gram.shape[0] // BLOCK
    eye = jnp.eye(BLOCK, dtype=jnp.float32)
    low, inv = {}, []
    rest = gram
    for k in range(count):
        diag = jnp.linalg.cholesky(rest[:BLOCK, :BLOCK], symmetrize_input=False)
        inverse = lax.linalg.triangular_solve(diag, eye, left_side=True, lower=True)
        inv.append(inverse)
        if k + 1 < count:
            panel = mm(rest[BLOCK:, :BLOCK], inverse, ((1,), (1,)), HIGH)
            for j in range(k + 1, count):
                low[j, k] = panel[(j - k - 1) * BLOCK : (j - k) * BLOCK]
            rest = rest[BLOCK:, BLOCK:] - mm(panel, panel, ((1,), (1,)), HIGH)
    return low, inv


def orthonormal(sketch, gram):
    low, inv = factor_blocks(gram)
    parts = []
    for k in range(len(inv)):
        right = sketch[:, k * BLOCK : (k + 1) * BLOCK]
        if k:
            row = jnp.concatenate([low[k, j] for j in range(k)], axis=1)
            right = right - mm(jnp.concatenate(parts, axis=1), row, ((1,), (1,)), HIGH)
        parts.append(mm(right, inv[k], ((1,), (1,)), HIGH))
    return jnp.concatenate(parts, axis=1).astype(jnp.bfloat16)


def project_kernel(
    depth, away_ref, home_ref, mine_ref, theirs_ref, out_ref,
    tiles, total, outgoing, incoming, relay,
    load_sem, x_send, x_recv, z_send, z_recv, keep_sem, core_send, core_recv,
):
    me = lax.axis_index("run")
    core, z = me % 2, me // 4
    flip = me + 1 - 2 * core
    across = me + 2 - 4 * ((me // 2) % 2)
    chunks, _, band, piece = total.shape
    rows = mine_ref.shape[0]
    last = depth - 1
    part = band // 2

    barrier = pltpu.get_barrier_semaphore()
    for device in (flip, across):
        pl.semaphore_signal(barrier, inc=1, device_id={"run": device}, device_id_type=MESH)

    @pl.when(z > 0)
    def _():
        pl.semaphore_signal(barrier, inc=1, device_id={"run": me - 4}, device_id_type=MESH)

    @pl.when(z < last)
    def _():
        pl.semaphore_signal(barrier, inc=1, device_id={"run": me + 4}, device_id_type=MESH)

    pl.semaphore_wait(barrier, 2 + (z + last - 1) // last + (2 * last - 1 - z) // last)

    def loads(k, slot):
        columns = pl.ds(pl.multiple_of(k * piece, piece), piece)
        return (
            pltpu.make_async_copy(
                mine_ref.at[:, columns], tiles.at[slot, pl.ds(0, rows)], load_sem.at[slot, 0]
            ),
            pltpu.make_async_copy(
                theirs_ref.at[:, columns], tiles.at[slot, pl.ds(rows, rows)], load_sem.at[slot, 1]
            ),
        )

    def x_copy(k):
        return pltpu.make_async_remote_copy(
            src_ref=outgoing.at[k], dst_ref=incoming.at[k],
            send_sem=x_send.at[k], recv_sem=x_recv.at[k],
            device_id={"run": across}, device_id_type=MESH,
        )

    def z_copy(k, slot, device):
        return pltpu.make_async_remote_copy(
            src_ref=relay.at[k, slot], dst_ref=relay.at[k, slot],
            send_sem=z_send.at[k, slot], recv_sem=z_recv.at[k, slot],
            device_id={"run": device}, device_id_type=MESH,
        )

    def result_copies(k):
        columns = pl.ds(pl.multiple_of((2 * k + core) * piece, piece), piece)
        keep = pltpu.make_async_copy(
            total.at[k, z, pl.ds(pl.multiple_of(core * part, part), part)],
            out_ref.at[:, columns], keep_sem.at[k],
        )
        give = pltpu.make_async_remote_copy(
            src_ref=total.at[k, z, pl.ds(pl.multiple_of((1 - core) * part, part), part)],
            dst_ref=out_ref.at[:, columns],
            send_sem=core_send.at[k], recv_sem=core_recv.at[k],
            device_id={"run": flip}, device_id_type=MESH,
        )
        return keep, give

    for copy in loads(0, 0):
        copy.start()

    def multiply(k, carry):
        slot = k % 2

        @pl.when(k + 1 < chunks)
        def _():
            for copy in loads(k + 1, 1 - slot):
                copy.start()

        for copy in loads(k, slot):
            copy.wait()

        def send_tile(i, carry):
            span = pl.ds(pl.multiple_of(i * TILE, TILE), TILE)
            value = jnp.dot(
                away_ref[...], tiles[slot, :, span], preferred_element_type=jnp.float32
            ).astype(jnp.bfloat16)
            for d in range(depth):
                outgoing[k, d, :, span] = value[d * band : (d + 1) * band]
            return carry

        def keep_tile(i, carry):
            span = pl.ds(pl.multiple_of(i * TILE, TILE), TILE)
            value = jnp.dot(home_ref[...], tiles[slot, :, span], preferred_element_type=jnp.float32)
            for d in range(depth):
                total[k, d, :, span] = value[d * band : (d + 1) * band]
            return carry

        lax.fori_loop(0, piece // TILE, send_tile, 0)
        x_copy(k).start()
        lax.fori_loop(0, piece // TILE, keep_tile, 0)
        return carry

    lax.fori_loop(0, chunks, multiply, 0)

    def pass_on(k, t, dest, slot, first, source, target):
        @pl.when(first)
        def _():
            relay[k, slot] = total[k, dest].astype(jnp.bfloat16)

        @pl.when(jnp.logical_not(first))
        def _():
            z_copy(k, slot, source).wait_recv()
            relay[k, slot] = (
                total[k, dest] + relay[k, slot].astype(jnp.float32)
            ).astype(jnp.bfloat16)

        z_copy(k, slot, target).start()

    def tick(now, carry):
        @pl.when(now < chunks)
        def _():
            x_copy(now).wait_recv()
            for d in range(depth):
                total[now, d] = total[now, d] + incoming[now, d].astype(jnp.float32)

        for t in range(last):
            k = now - t
            live = jnp.logical_and(k >= 0, k < chunks)

            @pl.when(jnp.logical_and(live, z <= t))
            def _():
                dest = last - t + z
                pass_on(k, t, dest, dest + 1, z == 0, me - 4, me + 4)

            @pl.when(jnp.logical_and(live, last - z <= t))
            def _():
                dest = t - last + z
                pass_on(k, t, dest, dest, z == last, me + 4, me - 4)

        @pl.when(now >= last)
        def _():
            k = now - last

            @pl.when(z > 0)
            def _():
                z_copy(k, z + 1, me - 4).wait_recv()
                total[k, z] = total[k, z] + relay[k, z + 1].astype(jnp.float32)

            @pl.when(z < last)
            def _():
                z_copy(k, z, me + 4).wait_recv()
                total[k, z] = total[k, z] + relay[k, z].astype(jnp.float32)

            for copy in result_copies(k):
                copy.start()

        return carry

    lax.fori_loop(0, chunks + last, tick, 0)

    def drain(k, carry):
        x_copy(k).wait_send()
        for t in range(last):
            @pl.when(z <= t)
            def _():
                z_copy(k, last - t + z + 1, me + 4).wait_send()

            @pl.when(last - z <= t)
            def _():
                z_copy(k, t - last + z, me - 4).wait_send()

        keep, give = result_copies(k)
        keep.wait()
        give.wait()
        return carry

    lax.fori_loop(0, chunks, drain, 0)


def project(depth, away, home, mine, theirs, piece):
    width, both = away.shape
    rows, columns = mine.shape
    chunks, band = columns // piece, width // depth
    any_space, vmem = pl.BlockSpec(memory_space=pl.ANY), pl.BlockSpec(memory_space=pltpu.VMEM)
    dma = pltpu.SemaphoreType.DMA
    return pl.pallas_call(
        functools.partial(project_kernel, depth),
        out_shape=jax.ShapeDtypeStruct((band // 2, 2 * columns), jnp.float32),
        in_specs=[vmem, vmem, any_space, any_space],
        out_specs=any_space,
        scratch_shapes=[
            pltpu.VMEM((2, both, piece), jnp.bfloat16),
            pltpu.VMEM((chunks, depth, band, piece), jnp.float32),
            pltpu.VMEM((chunks, depth, band, piece), jnp.bfloat16),
            pltpu.VMEM((chunks, depth, band, piece), jnp.bfloat16),
            pltpu.VMEM((chunks, depth + 1, band, piece), jnp.bfloat16),
            dma((2, 2)), dma((chunks,)), dma((chunks,)),
            dma((chunks, depth + 1)), dma((chunks, depth + 1)),
            dma((chunks,)), dma((chunks,)), dma((chunks,)),
        ],
        compiler_params=pltpu.CompilerParams(
            collective_id=0, has_side_effects=True, vmem_limit_bytes=60 * 2**20
        ),
        cost_estimate=pl.CostEstimate(
            flops=4 * width * both * columns, bytes_accessed=4 * rows * columns, transcendentals=0
        ),
    )(away, home, mine, theirs)


def solution(mesh):
    runs, entries = mesh.shape["run"], mesh.shape["entry"]
    depth = runs // 4

    def swap(value, bit, axis="run"):
        size = mesh.shape[axis]
        return lax.ppermute(value, axis, [(i, i ^ bit) for i in range(size)])

    def butterfly(value, axis):
        bit = 1
        while bit < mesh.shape[axis]:
            value = value + swap(value, bit, axis)
            bit *= 2
        return value

    def per_device(gradients, probes):
        me = lax.axis_index("run")
        core, x, z = me % 2, (me // 2) % 2, me // 4
        rows, columns = gradients.shape
        piece, width = probes.shape
        halves = runs // 2

        def columns_of(c):
            return jnp.concatenate(
                [
                    lax.dynamic_slice_in_dim(gradients, (2 * j + c) * piece, piece, 1)
                    for j in range(halves)
                ],
                axis=1,
            )

        theirs = swap(columns_of(1 - core), 1)
        mine = columns_of(core)
        table = lax.all_gather(probes, "run", axis=0, tiled=True)
        sketch = mm(gradients, table, ((1,), (0,)))
        sketch = butterfly(sketch, "entry")
        part = lax.axis_index("entry") % 2
        half = lax.dynamic_slice_in_dim(sketch, part * (width // 2), width // 2, 1)
        gram_half = butterfly(mm(sketch, half, ((0,), (0,)), HIGH), "run")
        far_half = swap(gram_half, 1, "entry")
        gram = jnp.concatenate(
            [
                jnp.where(part == 0, gram_half, far_half),
                jnp.where(part == 0, far_half, gram_half),
            ],
            axis=1,
        )
        basis = orthonormal(sketch, gram)
        basis_theirs = swap(basis, 1)

        band = width // depth // 2

        def bands(value, which):
            value = value.reshape(rows, depth, 2, band)
            return lax.dynamic_index_in_dim(value, which, 2, keepdims=False).reshape(
                rows, depth * band
            )

        both = jnp.concatenate
        away = both([bands(basis, 1 - x), bands(basis_theirs, 1 - x)]).T
        home = both([bands(basis, x), bands(basis_theirs, x)]).T
        return project(depth, away, home, mine, theirs, piece)

    placed = (P("run", "entry"), P(("entry", "run"), None))
    return jax.shard_map(
        per_device, mesh=mesh, in_specs=placed, out_specs=P("run", "entry"), check_vma=False
    )
```
